32 devices in a mesh: path: 16 (over z, y, core), fsdp: 2 (over x).
Axes of the slice: x: 2, y: 2, z: 4, core: 2. Of those that a mesh axis runs over, the one named last changes fastest.
Arguments:
- inputs: bfloat16 [16, 1536, 2048], P('path', 'fsdp'), may hold values from -6 to 6
- targets: bfloat16 [16, 1536, 2048], P('path', 'fsdp'), may hold values from -6 to 6
- token_ids: int32 [16, 1536], P('path', 'fsdp'), may hold values from 0 to 31999, as said below
- path_weights: bfloat16 [16, 2048, 2048], P('path', 'fsdp'), may hold values from -6 to 6
- stale_deltas: bfloat16 [16, 2048, 2048], P('path', 'fsdp'), may hold values from -6 to 6
- module_params: float32 [4, 2048, 2048], P(None, 'fsdp', 'path'), may hold values from -6 to 6
- momentum: float32 [4, 2048, 2048], P(None, 'fsdp', 'path'), may hold values from -3 to 3
- module_of_path: int32 [16], replicated, may hold values from 0 to 3, as said below
- sharing_counts: int32 [4], replicated, may hold values from 1 to 8, as said below
Outputs:
- next_weights: bfloat16 [16, 2048, 2048], P('path', 'fsdp')
- new_params: float32 [4, 2048, 2048], P(None, 'fsdp', 'path')
- new_momentum: float32 [4, 2048, 2048], P(None, 'fsdp', 'path')
The draws below stay inside these ranges and needn't reach their ends.
Inputs may be any that keep to these rules, and one draw needn't show every extreme that they name: `module_of_path`: every module is used by at least one path; one module is used by exactly 8 paths, every other by fewer. sharing_counts[m] is the number of paths p with module_of_path[p] = m. `token_ids`: each path's tokens with id 0 form a suffix that leaves at least a quarter of its 1536 tokens real.
All inputs are finite; a program needn't handle non-finite values.
Results may differ from the reference program's by a relative error of at most 0.015.
Values may be sent and summed in bfloat16 or wider, within the bound.
A program may use at most 128 MiB of HBM per device.

```python
import math
import jax
import jax.numpy as jnp
from jax import lax

DI = 2048
DO = 2048
MODULES = 4
VOCAB = 32000
TOK_DEV = 768
PATHS = 16
TOK_PATH = 1536
N_FSDP = 2


def incidence(key):
    fill_key, relabel_key, order_key = jax.random.split(key, 3)
    places = jnp.arange(PATHS, dtype=jnp.int32)
    half = PATHS // 2
    others = jax.random.randint(fill_key, (PATHS,), 1, MODULES).astype(jnp.int32)
    fixed = places - half + 1
    picked = jnp.where(places < half, 0, jnp.where(places < half + MODULES - 1, fixed, others))
    relabel = jax.random.permutation(relabel_key, MODULES)
    picked = relabel[picked]
    order = jax.random.permutation(order_key, PATHS)
    return picked[order].astype(jnp.int32)


def draw_module_of_path(key, part):
    return incidence(key)


def draw_sharing_counts(key, part):
    chosen = incidence(key)
    hits = (chosen[:, None] == jnp.arange(MODULES, dtype=jnp.int32)[None, :]).astype(jnp.int32)
    return jnp.sum(hits, axis=0).astype(jnp.int32)


def draw_token_ids(key, part):
    key = jax.random.fold_in(key, 7)
    length_key, id_key = jax.random.split(key)
    lengths = jax.random.randint(length_key, (PATHS, 1), TOK_PATH // 4 + 1, TOK_PATH + 1)
    values = jax.random.randint(id_key, (PATHS, TOK_PATH), 1, VOCAB)
    places = jnp.arange(TOK_PATH, dtype=jnp.int32)[None, :]
    return jnp.where(places < lengths, values, 0).astype(jnp.int32)


def block_levels(rng, shape, pieces, low, high):
    level, own = 1.0, jax.random.fold_in(rng, 6)
    for axis_at, blocks in pieces:
        steps = jnp.exp(jax.random.uniform(jax.random.fold_in(own, axis_at), (blocks,), jnp.float32, low / len(pieces), high / len(pieces)))
        level = level * jnp.repeat(steps, shape[axis_at] // blocks).reshape([-1 if axis == axis_at else 1 for axis in range(len(shape))])
    return level


def gaussian(rng, extent, scale, most, cuts=(), held_as=jnp.bfloat16):
    entries = scale * jax.random.normal(rng, extent, jnp.float32)
    if cuts:
        entries = entries * block_levels(rng, extent, cuts, -0.22, 0.18)
    return jnp.clip(entries, -most, most).astype(held_as)


def setup_inputs(seed: int = 0) -> dict:
    key_of = jax.random.split(jax.random.key(seed), 10)
    return {
        "inputs": gaussian(key_of[0], (PATHS, TOK_PATH, DI), 1.0, 6.0, ((0, 16), (1, 2))),
        "targets": gaussian(key_of[1], (PATHS, TOK_PATH, DO), 1.0, 6.0, ((0, 16), (1, 2))),
        "token_ids": draw_token_ids(jax.random.fold_in(key_of[9], 71), 0),
        "path_weights": gaussian(key_of[3], (PATHS, DI, DO), 1.0, 6.0, ((0, 16), (1, 2))),
        "stale_deltas": gaussian(key_of[4], (PATHS, DI, DO), 1.0, 6.0, ((0, 16), (1, 2))),
        "module_params": gaussian(key_of[5], (MODULES, DI, DO), 1.0, 6.0, ((1, 2), (2, 16)), jnp.float32),
        "momentum": gaussian(key_of[6], (MODULES, DI, DO), 0.5, 3.0, ((1, 2), (2, 16)), jnp.float32),
        "module_of_path": draw_module_of_path(jax.random.fold_in(key_of[9], 71), 0),
        "sharing_counts": draw_sharing_counts(jax.random.fold_in(key_of[9], 71), 0),
    }


def reference(inputs, targets, token_ids, path_weights, stale_deltas, module_params, momentum, module_of_path, sharing_counts):
    table = (module_of_path[:, None] == jnp.arange(MODULES, dtype=jnp.int32)[None, :]).astype(jnp.float32)

    def accumulate(total, items):
        row, delta = items
        return (total + row[:, None, None] * delta.astype(jnp.float32)[None], None)
    total, unused = lax.scan(accumulate, jnp.zeros((MODULES, DI, DO), jnp.float32), (table, stale_deltas))
    outer_grad = total / sharing_counts.astype(jnp.float32)[:, None, None]
    new_momentum = 0.9 * momentum + outer_grad
    outer_step = 0.7 * (outer_grad + 0.9 * new_momentum)
    new_params = module_params - outer_step
    outer_step_b = lax.optimization_barrier(outer_step.astype(jnp.bfloat16))

    def one_path(items):
        block_in, block_target, block_ids, weights, module = items
        values = block_in.astype(jnp.float32)
        scale = lax.rsqrt(lax.optimization_barrier(jnp.mean(values * values, axis=-1, keepdims=True)) + 1e-06)
        normed = (values * scale).astype(jnp.bfloat16)
        mask = (block_ids != 0).astype(jnp.float32)
        count = jnp.sum(mask)
        projected = jnp.dot(normed, weights, preferred_element_type=jnp.float32) / math.sqrt(DI)
        residual_rows = ((projected - block_target.astype(jnp.float32)) * mask[:, None]).astype(jnp.bfloat16)
        grad = jnp.zeros((DI, DO), jnp.float32)
        for block in range(N_FSDP):
            lower = block * TOK_DEV
            part = jnp.dot(normed[lower:lower + TOK_DEV].T, residual_rows[lower:lower + TOK_DEV], preferred_element_type=jnp.float32)
            part = lax.optimization_barrier(part.astype(jnp.bfloat16))
            grad = grad + part.astype(jnp.float32)
        grad = grad / jnp.sqrt(count)
        correction = outer_step_b[module].astype(jnp.float32)
        return (weights.astype(jnp.float32) - 0.25 * grad - correction).astype(jnp.bfloat16)
    next_weights = lax.map(one_path, (inputs, targets, token_ids, path_weights, module_of_path))
    return (next_weights, new_params, new_momentum)
```

```python
import functools
import math

import jax
import jax.numpy as jnp
from jax import lax
from jax.sharding import PartitionSpec as P


def per_device(
    paths,
    shards,
    inputs,
    targets,
    token_ids,
    path_weights,
    stale_deltas,
    module_params,
    momentum,
    module_of_path,
    sharing_counts,
):
    modules, rows, width = module_params.shape
    weights = path_weights[0]
    width_in = inputs.shape[-1]
    pair = shards == 2
    swap = [(0, 1), (1, 0)]

    if pair:
        other_weights = lax.ppermute(weights, "fsdp", swap)
    else:
        all_weights = lax.all_gather(weights, "fsdp", axis=0, tiled=True)

    delta = stale_deltas[0]
    sent = jnp.stack([delta[:, p * width : (p + 1) * width] for p in range(paths)])
    arrived = lax.all_to_all(sent, "path", 0, 0, tiled=True)
    labels = jnp.arange(modules, dtype=jnp.int32)
    hot = (labels[:, None] == module_of_path[None, :]).astype(jnp.float32)
    total = jnp.sum(hot[:, :, None, None] * arrived.astype(jnp.float32)[None], axis=1)
    outer_grad = total / sharing_counts.astype(jnp.float32)[:, None, None]
    new_momentum = 0.9 * momentum + outer_grad
    outer_step = 0.7 * (outer_grad + 0.9 * new_momentum)
    new_params = module_params - outer_step
    outer_step_b = outer_step.astype(jnp.bfloat16)

    steps = jnp.sum(
        jnp.where(hot[:, :, None, None] != 0, outer_step_b.astype(jnp.float32)[:, None], 0.0),
        axis=0,
    ).astype(jnp.bfloat16)
    steps = lax.all_to_all(steps, "path", 0, 0, tiled=True)
    correction = jnp.concatenate([steps[p] for p in range(paths)], axis=1)

    values = inputs[0].astype(jnp.float32)
    scale = lax.rsqrt(jnp.mean(values * values, axis=-1, keepdims=True) + 1e-06)
    normed = (values * scale).astype(jnp.bfloat16)
    mask = (token_ids[0] != 0).astype(jnp.float32)
    count = lax.psum(jnp.sum(mask), "fsdp")

    def product(a, b):
        return jnp.dot(a, b, preferred_element_type=jnp.float32)

    if pair:
        me = lax.axis_index("fsdp")
        own = lax.dynamic_slice_in_dim(normed, me * rows, rows, 1)
        far = lax.dynamic_slice_in_dim(normed, (1 - me) * rows, rows, 1)
        projected = product(own, weights) + product(far, other_weights)
    else:
        projected = product(normed, all_weights)
    projected = projected / math.sqrt(width_in)
    residual_rows = ((projected - targets[0].astype(jnp.float32)) * mask[:, None]).astype(
        jnp.bfloat16
    )

    def gradient(columns):
        return jnp.einsum(
            "ti,tj->ij", columns, residual_rows, preferred_element_type=jnp.float32
        ).astype(jnp.bfloat16)

    if pair:
        far_grad = lax.ppermute(gradient(far), "fsdp", swap)
        grad = gradient(own).astype(jnp.float32) + far_grad.astype(jnp.float32)
    else:
        grad = lax.psum_scatter(
            gradient(normed), "fsdp", scatter_dimension=0, tiled=True
        ).astype(jnp.float32)
    inner = weights.astype(jnp.float32) - 0.25 * (grad / jnp.sqrt(count))
    next_weights = (inner - correction.astype(jnp.float32)).astype(jnp.bfloat16)[None]
    return (next_weights, new_params, new_momentum)


def solution(mesh):
    return jax.shard_map(
        functools.partial(per_device, mesh.shape["path"], mesh.shape["fsdp"]),
        mesh=mesh,
        in_specs=(
            P("path", "fsdp", None),
            P("path", "fsdp", None),
            P("path", "fsdp"),
            P("path", "fsdp", None),
            P("path", "fsdp", None),
            P(None, "fsdp", "path"),
            P(None, "fsdp", "path"),
            P(),
            P(),
        ),
        out_specs=(P("path", "fsdp", None), P(None, "fsdp", "path"), P(None, "fsdp", "path")),
        check_vma=False,
    )
```

```python
import functools
import math

import jax
import jax.numpy as jnp
from jax import lax
from jax.experimental import pallas as pl
from jax.experimental.pallas import tpu as pltpu
from jax.sharding import PartitionSpec as P


def cost(flops, traffic):
    return pl.CostEstimate(flops=flops, bytes_accessed=traffic, transcendentals=0)


def split_columns(delta, paths):
    rows, columns = delta.shape
    width = columns // paths
    if width % 128:
        return jnp.stack([delta[:, p * width : (p + 1) * width] for p in range(paths)])

    def kernel(delta_ref, out_ref):
        out_ref[0] = delta_ref[...]

    return pl.pallas_call(
        kernel,
        grid=(paths,),
        in_specs=[pl.BlockSpec((rows, width), lambda p: (0, p))],
        out_specs=pl.BlockSpec((1, rows, width), lambda p: (p, 0, 0)),
        out_shape=jax.ShapeDtypeStruct((paths, rows, width), delta.dtype),
        cost_estimate=cost(0, 4 * delta.size),
    )(delta)


def outer_update(arrived, module_params, momentum, module_of_path, sharing_counts):
    paths, rows, width = arrived.shape
    modules = module_params.shape[0]
    tile = 128 if rows % 128 == 0 else rows

    def kernel(
        module_ref, count_ref, arrived_ref, params_ref, momentum_ref,
        params_out, momentum_out, steps_out, total,
    ):
        total[...] = jnp.zeros_like(total)
        for p in range(paths):
            m = module_ref[p]
            total[m] = total[m] + arrived_ref[p].astype(jnp.float32)
        for m in range(modules):
            shared = jnp.full((tile, width), count_ref[m], jnp.int32).astype(jnp.float32)
            outer_grad = total[m] / shared
            new_momentum = 0.9 * momentum_ref[m] + outer_grad
            outer_step = 0.7 * (outer_grad + 0.9 * new_momentum)
            params_out[m] = params_ref[m] - outer_step
            momentum_out[m] = new_momentum
            total[m] = outer_step
        for p in range(paths):
            steps_out[p] = total[module_ref[p]].astype(jnp.bfloat16)

    def block(n):
        return pl.BlockSpec((n, tile, width), lambda r: (0, r, 0))

    table = pl.BlockSpec(memory_space=pltpu.SMEM)
    state = jax.ShapeDtypeStruct(module_params.shape, jnp.float32)
    return pl.pallas_call(
        kernel,
        grid=(rows // tile,),
        in_specs=[table, table, block(paths), block(modules), block(modules)],
        out_specs=[block(modules), block(modules), block(paths)],
        out_shape=[state, state, jax.ShapeDtypeStruct(arrived.shape, jnp.bfloat16)],
        scratch_shapes=[pltpu.VMEM((modules, tile, width), jnp.float32)],
        compiler_params=pltpu.CompilerParams(vmem_limit_bytes=24 * 2**20),
        cost_estimate=cost(4 * arrived.size, 4 * arrived.size + 16 * module_params.size),
    )(module_of_path, sharing_counts, arrived, module_params, momentum)


def finish(weights, own_grad, far_grad, steps, count):
    paths, rows, width = steps.shape
    if width % 128:
        correction = jnp.concatenate([steps[p] for p in range(paths)], axis=1)
        grad = own_grad.astype(jnp.float32) + far_grad.astype(jnp.float32)
        inner = weights.astype(jnp.float32) - 0.25 * (grad / jnp.sqrt(count))
        return (inner - correction.astype(jnp.float32)).astype(jnp.bfloat16)

    def kernel(root_ref, weights_ref, own_ref, far_ref, steps_ref, out_ref):
        grad = own_ref[...].astype(jnp.float32) + far_ref[...].astype(jnp.float32)
        grad = grad / jnp.broadcast_to(root_ref[...], grad.shape)
        inner = weights_ref[...].astype(jnp.float32) - 0.25 * grad
        out_ref[...] = (inner - steps_ref[0].astype(jnp.float32)).astype(jnp.bfloat16)

    column = pl.BlockSpec((rows, width), lambda p: (0, p))
    return pl.pallas_call(
        kernel,
        grid=(paths,),
        in_specs=[
            pl.BlockSpec((1, width), lambda p: (0, 0)),
            column,
            column,
            column,
            pl.BlockSpec((1, rows, width), lambda p: (p, 0, 0)),
        ],
        out_specs=column,
        out_shape=jax.ShapeDtypeStruct(weights.shape, jnp.bfloat16),
        compiler_params=pltpu.CompilerParams(vmem_limit_bytes=24 * 2**20),
        cost_estimate=cost(6 * weights.size, 10 * weights.size),
    )(jnp.full((1, width), jnp.sqrt(count), jnp.float32), weights, own_grad, far_grad, steps)


def per_device(
    paths,
    shards,
    inputs,
    targets,
    token_ids,
    path_weights,
    stale_deltas,
    module_params,
    momentum,
    module_of_path,
    sharing_counts,
):
    rows = path_weights.shape[1]
    weights = path_weights[0]
    width_in = inputs.shape[-1]
    pair = shards == 2
    swap = [(0, 1), (1, 0)]

    mask = (token_ids[0] != 0).astype(jnp.float32)
    if pair:
        counted = jnp.full((8, 128), jnp.sum(mask), jnp.float32)
        count = (counted + lax.ppermute(counted, "fsdp", swap))[0, 0]
        other_weights = lax.ppermute(weights, "fsdp", swap)
    else:
        count = lax.psum(jnp.sum(mask), "fsdp")
        all_weights = lax.all_gather(weights, "fsdp", axis=0, tiled=True)

    arrived = lax.all_to_all(split_columns(stale_deltas[0], paths), "path", 0, 0, tiled=True)

    values = inputs[0].astype(jnp.float32)
    scale = lax.rsqrt(jnp.mean(values * values, axis=-1, keepdims=True) + 1e-06)
    normed = (values * scale).astype(jnp.bfloat16)

    def product(a, b):
        return jnp.dot(a, b, preferred_element_type=jnp.float32)

    if pair:
        me = lax.axis_index("fsdp")
        own = lax.dynamic_slice_in_dim(normed, me * rows, rows, 1)
        far = lax.dynamic_slice_in_dim(normed, (1 - me) * rows, rows, 1)
        projected = product(own, weights) + product(far, other_weights)
    else:
        projected = product(normed, all_weights)
    projected = projected / math.sqrt(width_in)
    residual_rows = ((projected - targets[0].astype(jnp.float32)) * mask[:, None]).astype(
        jnp.bfloat16
    )

    def gradient(columns):
        return jnp.einsum(
            "ti,tj->ij", columns, residual_rows, preferred_element_type=jnp.float32
        ).astype(jnp.bfloat16)

    if pair:
        sent_grad, arrived = lax.optimization_barrier((gradient(far), arrived))
        far_grad = lax.ppermute(sent_grad, "fsdp", swap)
        own_grad = gradient(own)
    else:
        own_grad = lax.psum_scatter(
            gradient(normed), "fsdp", scatter_dimension=0, tiled=True
        )
        far_grad = jnp.zeros_like(own_grad)

    new_params, new_momentum, steps = outer_update(
        arrived, module_params, momentum, module_of_path, sharing_counts
    )
    steps = lax.all_to_all(steps, "path", 0, 0, tiled=True)
    next_weights = finish(weights, own_grad, far_grad, steps, count)[None]
    return (next_weights, new_params, new_momentum)


def solution(mesh):
    return jax.shard_map(
        functools.partial(per_device, mesh.shape["path"], mesh.shape["fsdp"]),
        mesh=mesh,
        in_specs=(
            P("path", "fsdp", None),
            P("path", "fsdp", None),
            P("path", "fsdp"),
            P("path", "fsdp", None),
            P("path", "fsdp", None),
            P(None, "fsdp", "path"),
            P(None, "fsdp", "path"),
            P(),
            P(),
        ),
        out_specs=(P("path", "fsdp", None), P(None, "fsdp", "path"), P(None, "fsdp", "path")),
        check_vma=False,
    )
```

```python
import functools
import math

import jax
import jax.numpy as jnp
from jax import lax
from jax.experimental import pallas as pl
from jax.experimental.pallas import tpu as pltpu
from jax.sharding import PartitionSpec as P


def cost(flops, traffic):
    return pl.CostEstimate(flops=flops, bytes_accessed=traffic, transcendentals=0)


def split_columns(delta, paths):
    rows, columns = delta.shape
    width = columns // paths
    if width % 128:
        return jnp.stack([delta[:, p * width : (p + 1) * width] for p in range(paths)])

    group = math.gcd(paths, 4)

    def kernel(delta_ref, out_ref):
        for g in range(group):
            out_ref[g] = delta_ref[:, g * width : (g + 1) * width]

    return pl.pallas_call(
        kernel,
        grid=(paths // group,),
        in_specs=[pl.BlockSpec((rows, group * width), lambda p: (0, p))],
        out_specs=pl.BlockSpec((group, rows, width), lambda p: (p, 0, 0)),
        out_shape=jax.ShapeDtypeStruct((paths, rows, width), delta.dtype),
        compiler_params=pltpu.CompilerParams(vmem_limit_bytes=48 * 2**20),
        cost_estimate=cost(0, 4 * delta.size),
    )(delta)


def outer_update(arrived, module_params, momentum, module_of_path, sharing_counts):
    paths, rows, width = arrived.shape
    modules = module_params.shape[0]
    tile = 128 if rows % 128 == 0 else rows

    def kernel(
        module_ref, count_ref, arrived_ref, params_ref, momentum_ref,
        params_out, momentum_out, steps_out, total,
    ):
        total[...] = jnp.zeros_like(total)
        for p in range(paths):
            m = module_ref[p]
            total[m] = total[m] + arrived_ref[p].astype(jnp.float32)
        for m in range(modules):
            shared = jnp.full((tile, width), count_ref[m], jnp.int32).astype(jnp.float32)
            outer_grad = total[m] / shared
            new_momentum = 0.9 * momentum_ref[m] + outer_grad
            outer_step = 0.7 * (outer_grad + 0.9 * new_momentum)
            params_out[m] = params_ref[m] - outer_step
            momentum_out[m] = new_momentum
            total[m] = outer_step
        for p in range(paths):
            steps_out[p] = total[module_ref[p]].astype(jnp.bfloat16)

    def block(n):
        return pl.BlockSpec((n, tile, width), lambda r: (0, r, 0))

    table = pl.BlockSpec(memory_space=pltpu.SMEM)
    state = jax.ShapeDtypeStruct(module_params.shape, jnp.float32)
    return pl.pallas_call(
        kernel,
        grid=(rows // tile,),
        in_specs=[table, table, block(paths), block(modules), block(modules)],
        out_specs=[block(modules), block(modules), block(paths)],
        out_shape=[state, state, jax.ShapeDtypeStruct(arrived.shape, jnp.bfloat16)],
        scratch_shapes=[pltpu.VMEM((modules, tile, width), jnp.float32)],
        compiler_params=pltpu.CompilerParams(vmem_limit_bytes=48 * 2**20),
        cost_estimate=cost(4 * arrived.size, 4 * arrived.size + 16 * module_params.size),
    )(module_of_path, sharing_counts, arrived, module_params, momentum)


def finish(weights, own_grads, far_grads, steps, count):
    paths, rows, width = steps.shape
    parts = len(own_grads)
    if width % 128 or paths % parts:
        own_grad = jnp.concatenate(own_grads, axis=1)
        far_grad = jnp.concatenate(far_grads, axis=1)
        correction = jnp.concatenate([steps[p] for p in range(paths)], axis=1)
        grad = own_grad.astype(jnp.float32) + far_grad.astype(jnp.float32)
        inner = weights.astype(jnp.float32) - 0.25 * (grad / jnp.sqrt(count))
        return (inner - correction.astype(jnp.float32)).astype(jnp.bfloat16)

    group = math.gcd(paths // parts, 4)
    turns = paths // parts // group
    wide = group * width

    def kernel(root_ref, weights_ref, steps_ref, *refs):
        out_ref = refs[-1]
        root = jnp.broadcast_to(root_ref[...], (rows, width))
        for part in range(parts):
            own_ref, far_ref = refs[2 * part : 2 * part + 2]

            @pl.when(pl.program_id(0) // turns == part)
            def _():
                for g in range(group):
                    at = slice(g * width, (g + 1) * width)
                    grad = own_ref[:, at].astype(jnp.float32) + far_ref[:, at].astype(jnp.float32)
                    inner = weights_ref[:, at].astype(jnp.float32) - 0.25 * (grad / root)
                    new = inner - steps_ref[g].astype(jnp.float32)
                    out_ref[:, at] = new.astype(jnp.bfloat16)

    def within(part):
        return lambda p: (0, jnp.clip(p - part * turns, 0, turns - 1))

    column = pl.BlockSpec((rows, wide), lambda p: (0, p))
    pieces, grads = [], []
    for part in range(parts):
        pieces += [pl.BlockSpec((rows, wide), within(part))] * 2
        grads += [own_grads[part], far_grads[part]]
    return pl.pallas_call(
        kernel,
        grid=(parts * turns,),
        in_specs=[
            pl.BlockSpec((1, width), lambda p: (0, 0)),
            column,
            pl.BlockSpec((group, rows, width), lambda p: (p, 0, 0)),
            *pieces,
        ],
        out_specs=column,
        out_shape=jax.ShapeDtypeStruct(weights.shape, jnp.bfloat16),
        compiler_params=pltpu.CompilerParams(vmem_limit_bytes=48 * 2**20),
        cost_estimate=cost(6 * weights.size, 10 * weights.size),
    )(jnp.full((1, width), jnp.sqrt(count), jnp.float32), weights, steps, *grads)


def per_device(
    paths,
    shards,
    inputs,
    targets,
    token_ids,
    path_weights,
    stale_deltas,
    module_params,
    momentum,
    module_of_path,
    sharing_counts,
):
    rows = path_weights.shape[1]
    weights = path_weights[0]
    width_in = inputs.shape[-1]
    pair = shards == 2
    swap = [(0, 1), (1, 0)]

    mask = (token_ids[0] != 0).astype(jnp.float32)
    if pair:
        counted = jnp.full((8, 128), jnp.sum(mask), jnp.float32)
        count = (counted + lax.ppermute(counted, "fsdp", swap))[0, 0]
        half = weights.shape[1] // 2
        left, right = weights[:, :half], weights[:, half:]
        far_left = lax.ppermute(left, "fsdp", swap)
    else:
        count = lax.psum(jnp.sum(mask), "fsdp")
        all_weights = lax.all_gather(weights, "fsdp", axis=0, tiled=True)

    arrived = lax.all_to_all(split_columns(stale_deltas[0], paths), "path", 0, 0, tiled=True)

    values = inputs[0].astype(jnp.float32)
    scale = lax.rsqrt(jnp.mean(values * values, axis=-1, keepdims=True) + 1e-06)
    normed = (values * scale).astype(jnp.bfloat16)

    def product(a, b):
        return jnp.dot(a, b, preferred_element_type=jnp.float32)

    def residual(projected, wanted):
        projected = projected / math.sqrt(width_in)
        return ((projected - wanted.astype(jnp.float32)) * mask[:, None]).astype(jnp.bfloat16)

    def gradient(columns, residual_rows):
        return jnp.einsum(
            "ti,tj->ij", columns, residual_rows, preferred_element_type=jnp.float32
        ).astype(jnp.bfloat16)

    if pair:
        me = lax.axis_index("fsdp")
        own = lax.dynamic_slice_in_dim(normed, me * rows, rows, 1)
        far = lax.dynamic_slice_in_dim(normed, (1 - me) * rows, rows, 1)
        far_left, right_sent = lax.optimization_barrier((far_left, right))
        far_right = lax.ppermute(right_sent, "fsdp", swap)
        rest = residual(product(own, left) + product(far, far_left), targets[0, :, :half])
        left_sent, own_left = gradient(far, rest), gradient(own, rest)
        left_grad = lax.ppermute(left_sent, "fsdp", swap)
        rest = residual(product(own, right) + product(far, far_right), targets[0, :, half:])
        right_sent, own_left, count, arrived = lax.optimization_barrier(
            (gradient(far, rest), own_left, count, arrived)
        )
        right_grad = lax.ppermute(right_sent, "fsdp", swap)
        own_grads, far_grads = (own_left, gradient(own, rest)), (left_grad, right_grad)
    else:
        rest = residual(product(normed, all_weights), targets[0])
        own_grad = lax.psum_scatter(
            gradient(normed, rest), "fsdp", scatter_dimension=0, tiled=True
        )
        own_grads, far_grads = (own_grad,), (jnp.zeros_like(own_grad),)

    new_params, new_momentum, steps = outer_update(
        arrived, module_params, momentum, module_of_path, sharing_counts
    )
    steps = lax.all_to_all(steps, "path", 0, 0, tiled=True)
    next_weights = finish(weights, own_grads, far_grads, steps, count)[None]
    return (next_weights, new_params, new_momentum)


def solution(mesh):
    return jax.shard_map(
        functools.partial(per_device, mesh.shape["path"], mesh.shape["fsdp"]),
        mesh=mesh,
        in_specs=(
            P("path", "fsdp", None),
            P("path", "fsdp", None),
            P("path", "fsdp"),
            P("path", "fsdp", None),
            P("path", "fsdp", None),
            P(None, "fsdp", "path"),
            P(None, "fsdp", "path"),
            P(),
            P(),
        ),
        out_specs=(P("path", "fsdp", None), P(None, "fsdp", "path"), P(None, "fsdp", "path")),
        check_vma=False,
    )
```

```python
import functools
import math

import jax
import jax.numpy as jnp
from jax import lax
from jax.experimental import pallas as pl
from jax.experimental.pallas import tpu as pltpu
from jax.sharding import PartitionSpec as P


def cost(flops, traffic):
    return pl.CostEstimate(flops=flops, bytes_accessed=traffic, transcendentals=0)


def split_columns(delta, paths):
    rows, columns = delta.shape
    width = columns // paths
    if width % 128:
        return jnp.stack([delta[:, p * width : (p + 1) * width] for p in range(paths)])

    group = math.gcd(paths, 4)

    def kernel(delta_ref, out_ref):
        for g in range(group):
            out_ref[g] = delta_ref[:, g * width : (g + 1) * width]

    return pl.pallas_call(
        kernel,
        grid=(paths // group,),
        in_specs=[pl.BlockSpec((rows, group * width), lambda p: (0, p))],
        out_specs=pl.BlockSpec((group, rows, width), lambda p: (p, 0, 0)),
        out_shape=jax.ShapeDtypeStruct((paths, rows, width), delta.dtype),
        compiler_params=pltpu.CompilerParams(vmem_limit_bytes=48 * 2**20),
        cost_estimate=cost(0, 4 * delta.size),
    )(delta)


def outer_update(arrived, module_params, momentum, module_of_path, sharing_counts):
    paths, rows, width = arrived.shape
    modules = module_params.shape[0]
    tile = 128 if rows % 128 == 0 else rows

    def kernel(
        module_ref, count_ref, arrived_ref, params_ref, momentum_ref,
        params_out, momentum_out, steps_out, total,
    ):
        total[...] = jnp.zeros_like(total)
        for p in range(paths):
            m = module_ref[p]
            total[m] = total[m] + arrived_ref[p].astype(jnp.float32)
        for m in range(modules):
            shared = jnp.full((tile, width), count_ref[m], jnp.int32).astype(jnp.float32)
            outer_grad = total[m] / shared
            new_momentum = 0.9 * momentum_ref[m] + outer_grad
            outer_step = 0.7 * (outer_grad + 0.9 * new_momentum)
            params_out[m] = params_ref[m] - outer_step
            momentum_out[m] = new_momentum
            total[m] = outer_step
        for p in range(paths):
            steps_out[p] = total[module_ref[p]].astype(jnp.bfloat16)

    def block(n):
        return pl.BlockSpec((n, tile, width), lambda r: (0, r, 0))

    table = pl.BlockSpec(memory_space=pltpu.SMEM)
    state = jax.ShapeDtypeStruct(module_params.shape, jnp.float32)
    return pl.pallas_call(
        kernel,
        grid=(rows // tile,),
        in_specs=[table, table, block(paths), block(modules), block(modules)],
        out_specs=[block(modules), block(modules), block(paths)],
        out_shape=[state, state, jax.ShapeDtypeStruct(arrived.shape, jnp.bfloat16)],
        scratch_shapes=[pltpu.VMEM((modules, tile, width), jnp.float32)],
        compiler_params=pltpu.CompilerParams(vmem_limit_bytes=48 * 2**20),
        cost_estimate=cost(4 * arrived.size, 4 * arrived.size + 16 * module_params.size),
    )(module_of_path, sharing_counts, arrived, module_params, momentum)


def finish(weights, own_grads, far_grads, steps, count):
    paths, rows, width = steps.shape
    parts = len(own_grads)
    if width % 128 or paths % parts:
        own_grad = jnp.concatenate(own_grads, axis=1)
        far_grad = jnp.concatenate(far_grads, axis=1)
        correction = jnp.concatenate([steps[p] for p in range(paths)], axis=1)
        grad = own_grad.astype(jnp.float32) + far_grad.astype(jnp.float32)
        inner = weights.astype(jnp.float32) - 0.25 * (grad / jnp.sqrt(count))
        return (inner - correction.astype(jnp.float32)).astype(jnp.bfloat16)

    group = math.gcd(paths // parts, 4)
    turns = paths // parts // group
    wide = group * width

    def kernel(root_ref, weights_ref, steps_ref, *refs):
        out_ref = refs[-1]
        root = jnp.broadcast_to(root_ref[...], (rows, width))
        for part in range(parts):
            own_ref, far_ref = refs[2 * part : 2 * part + 2]

            @pl.when(pl.program_id(0) // turns == part)
            def _():
                for g in range(group):
                    at = slice(g * width, (g + 1) * width)
                    grad = own_ref[:, at].astype(jnp.float32) + far_ref[:, at].astype(jnp.float32)
                    inner = weights_ref[:, at].astype(jnp.float32) - 0.25 * (grad / root)
                    new = inner - steps_ref[g].astype(jnp.float32)
                    out_ref[:, at] = new.astype(jnp.bfloat16)

    def within(part):
        return lambda p: (0, jnp.clip(p - part * turns, 0, turns - 1))

    column = pl.BlockSpec((rows, wide), lambda p: (0, p))
    pieces, grads = [], []
    for part in range(parts):
        pieces += [pl.BlockSpec((rows, wide), within(part))] * 2
        grads += [own_grads[part], far_grads[part]]
    return pl.pallas_call(
        kernel,
        grid=(parts * turns,),
        in_specs=[
            pl.BlockSpec((1, width), lambda p: (0, 0)),
            column,
            pl.BlockSpec((group, rows, width), lambda p: (p, 0, 0)),
            *pieces,
        ],
        out_specs=column,
        out_shape=jax.ShapeDtypeStruct(weights.shape, jnp.bfloat16),
        compiler_params=pltpu.CompilerParams(vmem_limit_bytes=48 * 2**20),
        cost_estimate=cost(6 * weights.size, 10 * weights.size),
    )(jnp.full((1, width), jnp.sqrt(count), jnp.float32), weights, steps, *grads)


def per_device(
    paths,
    shards,
    inputs,
    targets,
    token_ids,
    path_weights,
    stale_deltas,
    module_params,
    momentum,
    module_of_path,
    sharing_counts,
):
    rows = path_weights.shape[1]
    weights = path_weights[0]
    width_in = inputs.shape[-1]
    pair = shards == 2
    swap = [(0, 1), (1, 0)]

    mask = (token_ids[0] != 0).astype(jnp.float32)
    if pair:
        counted = jnp.full((8, 128), jnp.sum(mask), jnp.float32)
        count = (counted + lax.ppermute(counted, "fsdp", swap))[0, 0]
        half = weights.shape[1] // 2
        left, right = weights[:, :half], weights[:, half:]
        far_left = lax.ppermute(left, "fsdp", swap)
    else:
        count = lax.psum(jnp.sum(mask), "fsdp")
        all_weights = lax.all_gather(weights, "fsdp", axis=0, tiled=True)

    arrived = lax.all_to_all(split_columns(stale_deltas[0], paths), "path", 0, 0, tiled=True)

    values = inputs[0].astype(jnp.float32)
    scale = lax.rsqrt(jnp.mean(values * values, axis=-1, keepdims=True) + 1e-06)
    normed = (values * scale).astype(jnp.bfloat16)

    def product(a, b):
        return jnp.dot(a, b, preferred_element_type=jnp.float32)

    def residual(projected, wanted):
        projected = projected / math.sqrt(width_in)
        return ((projected - wanted.astype(jnp.float32)) * mask[:, None]).astype(jnp.bfloat16)

    def gradient(columns, residual_rows):
        return jnp.einsum(
            "ti,tj->ij", columns, residual_rows, preferred_element_type=jnp.float32
        ).astype(jnp.bfloat16)

    if pair:
        me = lax.axis_index("fsdp")
        own = lax.dynamic_slice_in_dim(normed, me * rows, rows, 1)
        far = lax.dynamic_slice_in_dim(normed, (1 - me) * rows, rows, 1)
        far_left, right_sent = lax.optimization_barrier((far_left, right))
        far_right = lax.ppermute(right_sent, "fsdp", swap)
        rest = residual(product(own, left) + product(far, far_left), targets[0, :, :half])
        left_sent, own_left = gradient(far, rest), gradient(own, rest)
        far_right, left_ready = lax.optimization_barrier((far_right, left_sent))
        left_grad = lax.ppermute(left_ready, "fsdp", swap)
        rest = residual(product(own, right) + product(far, far_right), targets[0, :, half:])
        right_sent, own_left, count, arrived = lax.optimization_barrier(
            (gradient(far, rest), own_left, count, arrived)
        )
        right_grad = lax.ppermute(right_sent, "fsdp", swap)
        own_grads, far_grads = (own_left, gradient(own, rest)), (left_grad, right_grad)
    else:
        rest = residual(product(normed, all_weights), targets[0])
        own_grad = lax.psum_scatter(
            gradient(normed, rest), "fsdp", scatter_dimension=0, tiled=True
        )
        own_grads, far_grads = (own_grad,), (jnp.zeros_like(own_grad),)

    new_params, new_momentum, steps = outer_update(
        arrived, module_params, momentum, module_of_path, sharing_counts
    )
    steps = lax.all_to_all(steps, "path", 0, 0, tiled=True)
    next_weights = finish(weights, own_grads, far_grads, steps, count)[None]
    return (next_weights, new_params, new_momentum)


def solution(mesh):
    return jax.shard_map(
        functools.partial(per_device, mesh.shape["path"], mesh.shape["fsdp"]),
        mesh=mesh,
        in_specs=(
            P("path", "fsdp", None),
            P("path", "fsdp", None),
            P("path", "fsdp"),
            P("path", "fsdp", None),
            P("path", "fsdp", None),
            P(None, "fsdp", "path"),
            P(None, "fsdp", "path"),
            P(),
            P(),
        ),
        out_specs=(P("path", "fsdp", None), P(None, "fsdp", "path"), P(None, "fsdp", "path")),
        check_vma=False,
    )
```
